32 devices in a mesh: group: 2 (over x), dof: 16 (over z, y, core).
Axes of the slice: x: 2, y: 2, z: 4, core: 2. Of those that a mesh axis runs over, the one named last changes fastest.
Arguments:
- panel: bfloat16 [40960, 2048], P(('group', 'dof')), parts along dimension 0, as said below
- omega: bfloat16 [2048, 256], replicated, may hold values from -0.125 to 0.125
- psi: bfloat16 [256, 20480], P(None, 'dof'), may hold values from -0.0625 to 0.0625
- phi: bfloat16 [512, 20480], P(None, 'dof'), may hold values from -0.0390625 to 0.0390625
- theta: bfloat16 [512, 2048], replicated, may hold values from -0.125 to 0.125
Outputs:
- range_sketch: float32 [40960, 256], P(('group', 'dof')), parts along dimension 0
- corange_t: float32 [4096, 256], P(('group', 'dof')), parts along dimension 0
- core_sketch: float32 [1024, 512], P('group'), parts along dimension 0
The draws below stay inside these ranges and needn't reach their ends.
There are 2 independent parts, one for each index of `group`. The reference program is written for one: setup_inputs(seed, part) draws one part's arguments, and reference() takes and returns one part's arrays. A program takes and returns all parts, laid end to end along the dimension named above; an argument that names none is the same for every part. Nothing has to cross between parts.
Inputs may be any that keep to these rules, and one draw needn't show every extreme that they name: `panel`: real-valued record of order one.
All inputs are finite; a program needn't handle non-finite values.
Results may differ from the reference program's by a relative error of at most 0.0029.
Values sent between devices are 32-bit elements; how exact they have to be, the bound alone decides.
A program may use at most 64 MiB of HBM per device.

```python
import math
import jax
import jax.numpy as jnp
from jax import lax

SNAPS = 2048
RANK = 256
CORANGE = 256
CORE = 512
DOF = 20480


def draw_panel(key, part):
    key = jax.random.fold_in(key, 11)
    key_base, key_rows, key_cols = jax.random.split(key, 3)
    row_scale = jnp.exp(jax.random.uniform(key_rows, (DOF, 1), jnp.float32, math.log(0.3), math.log(3.0)))
    col_scale = jnp.exp(jax.random.uniform(key_cols, (1, SNAPS), jnp.float32, math.log(0.5), math.log(2.0)))
    base = jax.random.normal(key_base, (DOF, SNAPS), jnp.float32)
    return (base * row_scale * col_scale).astype(jnp.bfloat16)


def strengthened(entries, rng, source, target, shards_of, factor):
    owner, partner = [(jnp.arange(entries.shape[axis_at]) // (entries.shape[axis_at] // shards_of)).reshape([-1 if axis == axis_at else 1 for axis in range(entries.ndim)]) for axis_at in (source, target)]
    chosen = jax.random.permutation(rng, shards_of)[partner]
    strong = (owner == chosen) | (owner == (partner + shards_of // 2) % shards_of)
    return jnp.where(strong, factor * entries, entries)


def steps_of(own_key, shape, shards, least, largest):
    def one(dim, blocks):
        steps = jax.random.uniform(jax.random.fold_in(jax.random.fold_in(own_key, 6), dim), (blocks,), jnp.float32, least / len(shards), largest / len(shards))
        return jnp.repeat(jnp.exp(steps), shape[dim] // blocks).reshape((-1,) + (1,) * (len(shape) - dim - 1))

    gain = one(*shards[0])
    for cut in shards[1:]:
        gain = gain * one(*cut)
    return gain


def normal_values(own_key, dims, spread, bound, cuts=(), dtype=jnp.bfloat16):
    gain = steps_of(own_key, dims, cuts, -0.22, 0.18) if cuts else 1.0
    array = jax.random.normal(own_key, dims, jnp.float32) * spread * gain
    return jnp.minimum(jnp.maximum(array, -bound), bound).astype(dtype)


def gaussian_with(own_key, extent, scale, most, shards, heavy, kind=jnp.bfloat16):
    drawn = scale * jax.random.normal(own_key, extent, jnp.float32)
    if shards:
        drawn = drawn * steps_of(own_key, extent, shards, -0.22, 0.18)
    return jnp.clip(strengthened(drawn, jax.random.fold_in(own_key, 3), *heavy), -most, most).astype(kind)


def setup_inputs(seed: int = 0, part: int = 0) -> dict:
    splits = jax.random.split(jax.random.key(seed), 6)
    own_keys = jax.random.split(jax.random.fold_in(splits[5], part), 6)
    return {
        "panel": draw_panel(jax.random.fold_in(jax.random.fold_in(splits[5], part), 71), part),
        "omega": normal_values(splits[1], (SNAPS, RANK), SNAPS ** -0.5, 0.125),
        "psi": gaussian_with(splits[2], (CORANGE, DOF), DOF ** -0.5, 0.0625, ((1, 16),), (1, 0, 16, 2.0)),
        "phi": normal_values(splits[3], (CORE, DOF), DOF ** -0.5, 0.0390625, ((1, 16),)),
        "theta": normal_values(splits[4], (CORE, SNAPS), SNAPS ** -0.5, 0.125),
    }


def reference(panel, omega, psi, phi, theta):
    range_sketch = jnp.dot(panel, omega, preferred_element_type=jnp.float32)
    corange_t = lax.dot_general(panel, psi, (((0,), (1,)), ((), ())), preferred_element_type=jnp.float32)
    right = lax.dot_general(panel, theta, (((1,), (1,)), ((), ())), preferred_element_type=jnp.float32).astype(jnp.bfloat16)
    core_sketch = jnp.dot(phi, right, preferred_element_type=jnp.float32)
    return (range_sketch, corange_t, core_sketch)
```

```python
import functools

import jax
import jax.numpy as jnp
from jax import lax
from jax.experimental import pallas as pl
from jax.experimental.pallas import tpu as pltpu
from jax.sharding import PartitionSpec as P

F32 = jnp.float32
LANES = 128
COLS = 256


class Exchange:
    def __init__(self, me, order, buf, recv, send_sem, recv_sem, full=None):
        self.me, self.order, self.full = me, order, full
        self.buf, self.recv = buf, recv
        self.send_sem, self.recv_sem = send_sem, recv_sem
        self.rows = buf.shape[0]
        self.stages = len(order)
        self.offs = [0]
        for stage, bit in enumerate(order):
            mine = (me // (1 << bit)) % 2
            self.offs.append(self.offs[-1] + mine * (self.rows >> (stage + 1)))
        self.copies = []
        self.done = 0

    def partner(self, bit):
        mine = (self.me // (1 << bit)) % 2
        return self.me + (1 - 2 * mine) * (1 << bit)

    def _rows(self, off, size):
        return pl.ds(pl.multiple_of(off, 8), size)

    def _start(self, src, dst, bit):
        at = len(self.copies)
        copy = pltpu.make_async_remote_copy(
            src_ref=src, dst_ref=dst, send_sem=self.send_sem.at[at], recv_sem=self.recv_sem.at[at],
            device_id={"dof": self.partner(bit)}, device_id_type=pl.DeviceIdType.MESH)
        copy.start()
        self.copies.append(copy)

    def send(self):
        stage = len(self.copies)
        half = self.rows >> (stage + 1)
        if stage < self.stages:
            bit = self.order[stage]
            mine = (self.me // (1 << bit)) % 2
            src = self.buf.at[self._rows(self.offs[stage] + (1 - mine) * half, half)]
            dst = self.recv.at[pl.ds(self.rows - (self.rows >> stage), half)]
        else:
            stage = 2 * self.stages - 1 - stage
            bit = self.order[stage]
            size = self.rows >> (stage + 1)
            src = dst = self.full.at[self._rows(self.offs[stage + 1], size)]
        self._start(src, dst, bit)

    def advance(self):
        stage = self.done
        self.copies[stage].wait_recv()
        self.done += 1
        if stage < self.stages:
            half = self.rows >> (stage + 1)
            keep = self._rows(self.offs[stage + 1], half)
            came = pl.ds(self.rows - (self.rows >> stage), half)
            last = stage == self.stages - 1
            out = self.full if last and self.full is not None else self.buf
            out[keep] = self.buf[keep] + self.recv[came]
        if not self.finished():
            self.send()

    def finished(self):
        return self.done == self.stages * (2 if self.full is not None else 1)

    def drain(self):
        for copy in self.copies:
            copy.wait_send()


def position(device, order):
    at = 0
    for bit in order:
        at = 2 * at + (device >> bit) % 2
    return at


def kernel(n, orders_r, orders_c, panel_h, omega_h, psi_h, phi_h, theta_h, range_h, corange_h, core_h,
           panel, omega, psi, phi, theta, right, rng, rbuf, rrecv, cbuf, crecv, cfull,
           load_sem, out_sem, rsend, rrecv_sem, csend, crecv_sem):
    me = lax.axis_index("dof")
    bits = n.bit_length() - 1
    dof, snaps = panel.shape
    blocks = snaps // COLS
    nr, nc = len(orders_r), len(orders_c)
    own = snaps // n
    sub = own // nr
    core = phi.shape[0]

    loads = [pltpu.make_async_copy(psi_h, psi, load_sem.at[0])]
    for j in range(blocks):
        loads.append(pltpu.make_async_copy(
            panel_h.at[:, pl.ds(j * COLS, COLS)], panel.at[:, pl.ds(j * COLS, COLS)], load_sem.at[1 + j]))
    loads.append(pltpu.make_async_copy(theta_h, theta, load_sem.at[1 + blocks]))
    loads.append(pltpu.make_async_copy(phi_h, phi, load_sem.at[2 + blocks]))
    loads.append(pltpu.make_async_copy(omega_h, omega, load_sem.at[3 + blocks]))
    for load in loads:
        load.start()

    barrier = pltpu.get_barrier_semaphore()
    for bit in range(bits):
        mine = (me // (1 << bit)) % 2
        pl.semaphore_signal(barrier, inc=1, device_id={"dof": me + (1 - 2 * mine) * (1 << bit)},
                            device_id_type=pl.DeviceIdType.MESH)

    loads[0].wait()
    for j in range(blocks):
        loads[1 + j].wait()
        block = jnp.dot(psi[...], panel[:, j * COLS:(j + 1) * COLS], preferred_element_type=F32).T
        for k in range(COLS // sub):
            row = j * COLS + k * sub
            device, chunk = row // own, (row % own) // sub
            at = position(device, orders_r[chunk]) * sub
            rbuf[chunk, at:at + sub, :] = block[k * sub:(k + 1) * sub, :]

    pl.semaphore_wait(barrier, bits)
    xr = [Exchange(me, order, rbuf.at[c], rrecv.at[c], rsend.at[c], rrecv_sem.at[c])
          for c, order in enumerate(orders_r)]
    xc = [Exchange(me, order, cbuf.at[c], crecv.at[c], csend.at[c], crecv_sem.at[c], cfull.at[c])
          for c, order in enumerate(orders_c)]
    for x in xr:
        x.send()

    loads[1 + blocks].wait()
    tile = 256

    def right_tile(i, _):
        rows = pl.ds(pl.multiple_of(i * tile, tile), tile)
        right[rows, :] = lax.dot_general(
            panel[rows, :], theta[...], (((1,), (1,)), ((), ())), preferred_element_type=F32).astype(right.dtype)
        return _

    tiles = dof // tile
    lax.fori_loop(0, tiles // 2, right_tile, 0)
    xr[0].advance()
    xr[-1].advance()
    lax.fori_loop(tiles // 2, tiles, right_tile, 0)

    loads[2 + blocks].wait()
    per = core // LANES // nc
    for c in range(nc):
        part = jnp.dot(phi[...], right[:, c * per * LANES:(c + 1) * per * LANES], preferred_element_type=F32)
        for g in range(per):
            cbuf[c, g * core:(g + 1) * core, :] = part[:, g * LANES:(g + 1) * LANES]
        xc[c].send()
    for x in xr[1:-1]:
        x.advance()
    for x in xc:
        x.advance()

    loads[3 + blocks].wait()

    def range_tile(i, _):
        rows = pl.ds(pl.multiple_of(i * tile, tile), tile)
        rng[rows, :] = jnp.dot(panel[rows, :], omega[...], preferred_element_type=F32)
        return _

    lax.fori_loop(0, tiles, range_tile, 0)
    outs = [pltpu.make_async_copy(rng, range_h, out_sem.at[0])]
    outs[0].start()

    def finish_r(c):
        x = xr[c]
        copy = pltpu.make_async_copy(
            x.buf.at[x._rows(x.offs[-1], sub)], corange_h.at[pl.ds(c * sub, sub)], out_sem.at[1 + c])
        copy.start()
        outs.append(copy)

    def finish_c(c):
        for g in range(per):
            copy = pltpu.make_async_copy(
                xc[c].full.at[pl.ds(g * core, core)], core_h.at[:, pl.ds((c * per + g) * LANES, LANES)],
                out_sem.at[1 + nr + c * per + g])
            copy.start()
            outs.append(copy)

    while not all(x.finished() for x in xr + xc):
        for c, x in enumerate(xc):
            if not x.finished():
                x.advance()
                if x.finished():
                    finish_c(c)
        for c, x in enumerate(xr):
            if not x.finished():
                x.advance()
                if x.finished():
                    finish_r(c)
    for x in xr + xc:
        x.drain()
    for copy in outs:
        copy.wait()


def body(n, panel, omega, psi, phi, theta):
    dof, snaps = panel.shape
    rank, corange, core = omega.shape[1], psi.shape[0], phi.shape[0]
    bits = n.bit_length() - 1
    order_a = tuple(range(bits))
    order_b = (0, 2, 1) + tuple(range(3, bits)) if bits > 2 else order_a
    nr = min(4, snaps // n // 8)
    nc = min(4, core * core // LANES // n // 8)
    orders_r = (order_a,) * (nr - 1) + (order_b,)
    orders_c = (order_a,) * (nc - 1) + (order_b,)
    rrows, crows = snaps // nr, core * core // LANES // nc
    blocks = snaps // COLS
    any_space = pl.BlockSpec(memory_space=pl.ANY)
    dma = pltpu.SemaphoreType.DMA
    return pl.pallas_call(
        functools.partial(kernel, n, orders_r, orders_c),
        out_shape=(
            jax.ShapeDtypeStruct((dof, rank), F32),
            jax.ShapeDtypeStruct((snaps // n, corange), F32),
            jax.ShapeDtypeStruct((core, core), F32),
        ),
        in_specs=[any_space] * 5,
        out_specs=(any_space,) * 3,
        scratch_shapes=[
            pltpu.VMEM(panel.shape, panel.dtype),
            pltpu.VMEM(omega.shape, omega.dtype),
            pltpu.VMEM(psi.shape, psi.dtype),
            pltpu.VMEM(phi.shape, phi.dtype),
            pltpu.VMEM(theta.shape, theta.dtype),
            pltpu.VMEM((dof, core), jnp.bfloat16),
            pltpu.VMEM((dof, rank), F32),
            pltpu.VMEM((nr, rrows, corange), F32),
            pltpu.VMEM((nr, rrows, corange), F32),
            pltpu.VMEM((nc, crows, LANES), F32),
            pltpu.VMEM((nc, crows, LANES), F32),
            pltpu.VMEM((nc, crows, LANES), F32),
            dma((4 + blocks,)),
            dma((1 + nr + core // LANES,)),
            dma((nr, bits)),
            dma((nr, bits)),
            dma((nc, 2 * bits)),
            dma((nc, 2 * bits)),
        ],
        compiler_params=pltpu.CompilerParams(
            collective_id=0, has_side_effects=True, vmem_limit_bytes=40 * 1024 * 1024),
        cost_estimate=pl.CostEstimate(
            flops=2 * dof * snaps * (rank + corange + core) + 2 * dof * core * core,
            bytes_accessed=2 * dof * snaps * 2, transcendentals=0),
        name="sketches",
    )(panel, omega, psi, phi, theta)


def solution(mesh):
    in_specs = (P(("group", "dof"), None), P(), P(None, "dof"), P(None, "dof"), P())
    out_specs = (P(("group", "dof"), None), P(("group", "dof"), None), P("group", None))
    return jax.shard_map(functools.partial(body, mesh.shape["dof"]), mesh=mesh, in_specs=in_specs,
                         out_specs=out_specs, check_vma=False)
```
